32 devices in a mesh: fsdp: 16 (over z, x, core), tp: 2 (over y).
Axes of the slice: x: 2, y: 2, z: 4, core: 2. Of those that a mesh axis runs over, the one named last changes fastest.
Arguments:
- tokens: bfloat16 [8192, 768], P(('fsdp', 'tp')), may hold values from -6 to 6
- lengths: int32 [16], replicated, may hold values from 288 to 512, as said below
- routes: int32 [8192, 1], P('fsdp'), may hold values from 0 to 3; in each aligned block of 512 rows (0 to 511, 512 to 1023, ...) at most 192 rows name the same one
- cotangent: bfloat16 [8192, 768], P(('fsdp', 'tp')), may hold values from -6 to 6
- gain_attn: bfloat16 [768], replicated, may hold values from 0.5 to 1.5
- gain_moe: bfloat16 [768], replicated, may hold values from 0.5 to 1.5
- qkv_weight: bfloat16 [768, 3, 768], P('fsdp', None, 'tp'), may hold values from -0.21875 to 0.21875
- out_weight: bfloat16 [768, 768], P('fsdp', 'tp'), may hold values from -1.75 to 1.75
- rel_table: bfloat16 [32, 12], replicated, may hold values from -4 to 4
- router_weight: bfloat16 [768, 4], replicated, may hold values from -0.15625 to 0.15625
- w_in: bfloat16 [768, 4, 3072], P('fsdp', None, 'tp'), may hold values from -0.21875 to 0.21875
- w_out: bfloat16 [768, 4, 3072], P('fsdp', None, 'tp'), may hold values from -0.625 to 0.625
Outputs:
- mixed: bfloat16 [8192, 768], P(('fsdp', 'tp'))
- balance: float32 [], replicated
- grad_tokens: bfloat16 [8192, 768], P(('fsdp', 'tp'))
- grad_gain_attn: float32 [768], replicated
- grad_gain_moe: float32 [768], replicated
- grad_qkv: float32 [768, 3, 768], P('fsdp', None, 'tp')
- grad_out: float32 [768, 768], P('fsdp', 'tp')
- grad_table: float32 [32, 12], replicated
- grad_router: float32 [768, 4], replicated
- grad_in: float32 [768, 4, 3072], P('fsdp', None, 'tp')
- grad_down: float32 [768, 4, 3072], P('fsdp', None, 'tp')
The draws below stay inside these ranges and needn't reach their ends.
Inputs may be any that keep to these rules, and one draw needn't show every extreme that they name: `lengths`: some sequence has exactly 512 real tokens. `routes`: in each aligned block of 512 rows (one sequence) no expert is named by more than 192 rows, a bound that some block reaches.
All inputs are finite; a program needn't handle non-finite values.
Results may differ from the reference program's by a relative error of at most 0.017.
Values may be sent and summed in bfloat16 or wider, within the bound.
A program may use at most 192 MiB of HBM per device.

```python
import math
import jax
import jax.numpy as jnp
import numpy as np
from jax import lax

D = 768
HEADS = 12
HD = 64
FF = 3072
BUCKETS = 32
EXP = 4
SEQ = 512
CAP = 192
TOKENS = 8192
N_FSDP = 16


def draw_lengths(key, part):
    key = jax.random.fold_in(key, 7)
    first_key, second_key = jax.random.split(key)
    drawn = jax.random.randint(first_key, (N_FSDP,), SEQ // 2 + SEQ // 16, SEQ + 1)
    longest = jax.random.randint(second_key, (), 0, N_FSDP)
    return jnp.where(jnp.arange(N_FSDP) == longest, SEQ, drawn).astype(jnp.int32)


def with_spikes(values, rng, source, target, shards_of, factor):
    def block_of(position):
        return (jnp.arange(values.shape[position]) // (values.shape[position] // shards_of)).reshape((-1,) + (1,) * (values.ndim - 1 - position))

    near = jax.random.permutation(rng, shards_of)[block_of(target)]
    far = (block_of(target) + shards_of // 2) % shards_of
    return jnp.where((block_of(source) == near) | (block_of(source) == far), factor * values, values)


def level_of(own_key, dims, shards, low, high):
    loudness = 1.0
    for axis_at, blocks in shards:
        draws = jax.random.uniform(jax.random.fold_in(jax.random.fold_in(own_key, 6), axis_at), (blocks,), jnp.float32, low / len(shards), high / len(shards))
        loudness = loudness * jnp.repeat(jnp.exp(draws), dims[axis_at] // blocks).reshape((-1,) + (1,) * (len(dims) - 1 - axis_at))
    return loudness


def assign_block(rng, own, number, rows, count, top, reach, lean):
    order = jax.random.permutation(rng, count)
    heavy_load, common = load_shares(count, rows * top, reach, lean, True), load_shares(count, rows * top, reach, lean, False)
    places = jnp.arange(count)

    def named(sizes, offset_by):
        used = int((sizes > 0).sum())
        fixed = max(1, used // 4)
        shifted = fixed + (places - fixed + offset_by * (used - fixed)) % max(1, count - fixed)
        return jnp.zeros((count,), jnp.int32).at[order[jnp.where(places < fixed, places, shifted)]].set(jnp.asarray(sizes, jnp.int32))

    sizes = jnp.where(number % 4 == 0, named(heavy_load, number // 4), named(common, number - number // 4 - 1))
    mixed = jax.random.permutation(jax.random.fold_in(own, 3), count)
    source_of, taker = mixed[0:count // 2 * 2:2], mixed[1:count // 2 * 2:2]
    slack = jnp.minimum(sizes[source_of] - 1, reach - sizes[taker]) // 2
    slack = jnp.where((source_of == order[0]) | (taker == order[0]) | (sizes[taker] == 0), 0, jnp.maximum(slack, 0))
    shifted = jax.random.randint(jax.random.fold_in(own, 4), (count // 2,), 0, 1 << 20) % (slack + 1)
    sizes = sizes.at[source_of].add(-shifted).at[taker].add(shifted)
    items = jnp.searchsorted(jnp.cumsum(sizes), jnp.arange(rows * top), side="right").astype(jnp.int32)
    grid = items.reshape(top, rows).T
    grid = grid[jax.random.permutation(jax.random.fold_in(own, 1), rows)]
    offset_by = jax.random.randint(jax.random.fold_in(own, 2), (rows, 1), 0, top)
    return jnp.take_along_axis(grid, (jnp.arange(top)[None, :] + offset_by) % top, axis=1)


def load_shares(number_of, total, reach, slope, full):
    portions = [(1 << 20) // math.isqrt(grade ** slope) + 1 for grade in range(1, number_of + 1)]
    largest = reach if full else min(reach, max(-(-total // number_of), total * portions[0] // sum(portions)))
    least = 1 if total - largest >= number_of - 1 else 0
    holding, rest = [largest] + [least] * (number_of - 1), total - largest - least * (number_of - 1)
    while rest > 0:
        movable = [i for i in range(1, number_of) if holding[i] < largest] or [i for i in range(1, number_of) if holding[i] < reach]
        whole, budget = sum([portions[i] for i in movable]), rest
        for i in movable:
            extra = min(reach - holding[i], max(1, budget * portions[i] // whole), rest)
            holding[i] = holding[i] + extra
            rest = rest - extra
    return np.array(holding)


def normal_values(rng, shape, width, reach, shards=(), kind=jnp.bfloat16):
    gain = level_of(rng, shape, shards, -0.22, 0.18) if shards else 1.0
    array = jax.random.normal(rng, shape, jnp.float32) * width * gain
    return jnp.minimum(jnp.maximum(array, -reach), reach).astype(kind)


def bell_draw_with(stream_key, shape, scale, reach, shards, heavy, kind=jnp.bfloat16):
    entries = scale * jax.random.normal(stream_key, shape, jnp.float32)
    if shards:
        entries = entries * level_of(stream_key, shape, shards, -0.22, 0.18)
    return jnp.clip(with_spikes(entries, jax.random.fold_in(stream_key, 3), *heavy), -reach, reach).astype(kind)


def setup_inputs(seed: int = 0) -> dict:
    arg_keys = jax.random.split(jax.random.key(seed), 13)
    tokens = bell_draw_with(arg_keys[0], (TOKENS, D), 1.0, 6.0, ((0, 32),), (0, 1, 32, 2.75))
    lengths = draw_lengths(jax.random.fold_in(arg_keys[12], 71), 0)
    routes_keys = jax.random.split(jax.random.fold_in(arg_keys[2], 1), TOKENS // SEQ)
    routes_turns = jax.random.permutation(jax.random.fold_in(arg_keys[2], 3), TOKENS // SEQ)
    routes = jax.vmap(lambda own, number: assign_block(jax.random.fold_in(arg_keys[2], 2), own, number, SEQ, EXP, 1, CAP, 2))(routes_keys, routes_turns).reshape((TOKENS, 1))
    cotangent = bell_draw_with(arg_keys[3], (TOKENS, D), 1.0, 6.0, ((0, 32),), (0, 1, 32, 2.75))
    gain_attn = jnp.clip(1.0 + 0.1 * jax.random.normal(arg_keys[4], (D,), jnp.float32), 0.5, 1.5).astype(jnp.bfloat16)
    gain_moe = jnp.clip(1.0 + 0.1 * jax.random.normal(arg_keys[5], (D,), jnp.float32), 0.5, 1.5).astype(jnp.bfloat16)
    qkv_weight = normal_values(arg_keys[6], (D, 3, D), D ** -0.5, 0.21875, ((0, 16), (2, 2)))
    out_weight = normal_values(arg_keys[7], (D, D), (max(4, D * 8 // SEQ)) ** -0.5, 1.75, ((0, 16), (1, 2)))
    rel_table = normal_values(arg_keys[8], (BUCKETS, HEADS), 1.0, 4.0)
    router_weight = normal_values(arg_keys[9], (D, EXP), (2 * D) ** -0.5, 0.15625)
    w_in = normal_values(arg_keys[10], (D, EXP, FF), D ** -0.5, 0.21875, ((0, 16), (2, 2)))
    w_out = normal_values(arg_keys[11], (D, EXP, FF), (FF // 32) ** -0.5, 0.625, ((0, 16), (2, 2)))
    return {"tokens": tokens, "lengths": lengths, "routes": routes, "cotangent": cotangent, "gain_attn": gain_attn, "gain_moe": gain_moe, "qkv_weight": qkv_weight, "out_weight": out_weight, "rel_table": rel_table, "router_weight": router_weight, "w_in": w_in, "w_out": w_out}


@jax.custom_vjp
def low(v):
    return lax.optimization_barrier(v.astype(jnp.bfloat16)).astype(jnp.float32)

@jax.custom_vjp
def low_back(v):
    return v

def low_keep(v):
    return (low(v), None)

def low_pass(kept, grad):
    return (grad,)

def back_keep(v):
    return (v, None)

def back_low(kept, grad):
    return (low(grad),)
low.defvjp(low_keep, low_pass)
low_back.defvjp(back_keep, back_low)
epsilon = 1e-06
balance_weight = 0.01
far_edges = (12, 16, 23, 32, 46, 64, 91)
highest = lax.Precision.HIGHEST

def bucket_index(query_pos, key_pos):
    offset = key_pos[None, :] - query_pos[:, None]
    spread = jnp.abs(offset)
    far_bucket = 8 + sum(((spread >= edge).astype(jnp.int32) for edge in far_edges))
    near_bucket = jnp.where(spread < 8, spread, far_bucket)
    return near_bucket + jnp.where(offset > 0, 16, 0).astype(jnp.int32)

def rms_norm(values, gain_vec):
    factor = lax.rsqrt(lax.optimization_barrier(jnp.mean(values * values, axis=-1, keepdims=True)) + epsilon)
    return values * factor * gain_vec

def group_forward(params, group_tokens, length, group_routes):
    gain_attn, gain_moe, qkv_weight, out_weight, rel_table, router_weight, w_in, w_out = params
    positions = jnp.arange(SEQ, dtype=jnp.int32)
    valid_int = (positions < length).astype(jnp.int32)
    valid = valid_int.astype(jnp.float32)[:, None]
    normed_attn = low(rms_norm(group_tokens, gain_attn))
    qkv = low_back(low(jnp.einsum('sd,dch->csh', normed_attn, qkv_weight, precision=highest)))
    heads = qkv.reshape(3, SEQ, HEADS, HD).transpose(0, 2, 1, 3)
    bias_full = jnp.transpose(rel_table[bucket_index(positions, positions)], (2, 0, 1))
    scores = jnp.einsum('hqe,hke->hqk', heads[0], heads[1], precision=highest) * (1.0 / math.sqrt(HD)) + bias_full
    scores = jnp.where(valid_int[None, None, :] > 0, low_back(scores), -jnp.inf)
    attn_probs = jax.nn.softmax(scores, axis=-1)
    context = jnp.einsum('hqk,hke->hqe', low(attn_probs), heads[2], precision=highest)
    context = low_back(low(context)).transpose(1, 0, 2).reshape(SEQ, D)
    branch = low_back(jnp.dot(context, out_weight.T, precision=highest)) * valid
    mid = group_tokens + branch
    normed_moe = low(rms_norm(mid, gain_moe))
    router_probs = jax.nn.softmax(jnp.dot(normed_moe, router_weight, precision=highest), axis=-1)
    expert_ids = jnp.arange(EXP, dtype=jnp.int32)
    chosen = (group_routes[:, None] == expert_ids[None, :]).astype(jnp.int32)
    gate = lax.optimization_barrier(jnp.sum(router_probs * chosen.astype(jnp.float32), axis=1, keepdims=True))
    live = chosen * valid_int[:, None]
    slot_ids = lax.optimization_barrier(jnp.sum(live * (jnp.cumsum(live, axis=0) - 1), axis=1))
    flat_index = jnp.where(valid_int > 0, group_routes * CAP + slot_ids, EXP * CAP).astype(jnp.int32)
    dispatched = jnp.zeros((EXP * CAP + 1, D), jnp.float32).at[flat_index].add(normed_moe)[:EXP * CAP]
    pre_act = low_back(jnp.einsum('ecd,def->ecf', dispatched.reshape(EXP, CAP, D), w_in, precision=highest))
    act = low(jax.nn.gelu(pre_act, approximate=False))
    expert_out = low_back(jnp.einsum('ecf,def->ecd', act, w_out, precision=highest))
    padded = jnp.concatenate([expert_out.reshape(EXP * CAP, D), jnp.zeros((1, D), jnp.float32)], axis=0)
    moe_branch = gate * padded[flat_index] * valid
    return (mid + moe_branch, lax.optimization_barrier(jnp.sum(valid * router_probs, axis=0)))

def reference(tokens, lengths, routes, cotangent, gain_attn, gain_moe, qkv_weight, out_weight, rel_table, router_weight, w_in, w_out):
    route_rows = routes.reshape(N_FSDP, SEQ)
    positions = jnp.arange(SEQ, dtype=jnp.int32)
    valid_all = (positions[None, :] < lengths[:, None]).astype(jnp.float32)
    chosen_all = (route_rows[:, :, None] == jnp.arange(EXP, dtype=jnp.int32)[None, None, :]).astype(jnp.float32)
    counts = lax.optimization_barrier(jnp.sum(chosen_all * valid_all[:, :, None], axis=(0, 1)))
    total_tokens = jnp.sum(lengths).astype(jnp.float32)
    fraction = counts / total_tokens

    def forward(token_rows, *params):

        def one_group(carry, inputs):
            group_tokens, length, group_routes = inputs
            mixed_rows, prob_sums = jax.checkpoint(group_forward)(params, group_tokens, length, group_routes)
            return (carry + prob_sums, mixed_rows)
        prob_total, mixed_groups = lax.scan(one_group, jnp.zeros((EXP,), jnp.float32), (token_rows.reshape(N_FSDP, SEQ, D), lengths, route_rows))
        balance = EXP * jnp.sum(fraction * (prob_total / total_tokens))
        return (mixed_groups.reshape(TOKENS, D), balance)
    floats = tuple((source.astype(jnp.float32) for source in (tokens, gain_attn, gain_moe, qkv_weight, out_weight, rel_table, router_weight, w_in, w_out)))
    (mixed, balance), pull_back = jax.vjp(forward, *floats)
    grads = pull_back((cotangent.astype(jnp.float32), jnp.asarray(balance_weight, jnp.float32)))
    return (mixed.astype(jnp.bfloat16), balance, grads[0].astype(jnp.bfloat16), grads[1], grads[2], grads[3], grads[4], grads[5], grads[6], grads[7], grads[8])
```

```python
import math

import jax
import jax.numpy as jnp
from jax import lax
from jax.experimental import pallas as pl
from jax.experimental.pallas import tpu as pltpu
from jax.sharding import PartitionSpec as P

HEADS = 12
HD = 64
BUCKETS = 32
EXP = 4


epsilon = 1e-06
balance_weight = 0.01
far_edges = (12, 16, 23, 32, 46, 64, 91)
highest = lax.Precision.HIGHEST


def bucket_index(query_pos, key_pos):
    offset = key_pos[None, :] - query_pos[:, None]
    spread = jnp.abs(offset)
    far_bucket = 8 + sum(((spread >= edge).astype(jnp.int32) for edge in far_edges))
    near_bucket = jnp.where(spread < 8, spread, far_bucket)
    return near_bucket + jnp.where(offset > 0, 16, 0).astype(jnp.int32)


def norm_rows(values, gain_vec):
    factor = lax.rsqrt(jnp.mean(values * values, axis=-1, keepdims=True) + epsilon)
    hat_rows = values * factor
    return (hat_rows, factor, (hat_rows * gain_vec).astype(jnp.bfloat16))


def norm_back(grad_normed, hat_rows, factor, gain_vec):
    grad_hat = grad_normed * gain_vec
    inner = jnp.mean(grad_hat * hat_rows, axis=-1, keepdims=True)
    return (factor * (grad_hat - hat_rows * inner), jnp.sum(grad_normed * hat_rows, axis=0))


PAIR = 2 * HD
vmem_bytes = 40 * 1024 * 1024


def offset_buckets(seq_len):
    places = jnp.arange(2 * seq_len, dtype=jnp.int32)
    offset = jnp.where(places < seq_len, places, places - 2 * seq_len)
    return bucket_index(jnp.zeros((1,), jnp.int32), offset)[0]


def attn_forward_kernel(len_ref, query_ref, key_ref, value_ref, table_ref, context_ref, probs_ref):
    seq_len = query_ref.shape[0]
    key_pos = lax.broadcasted_iota(jnp.int32, (1, seq_len), 1)
    key_valid = key_pos < len_ref[0]
    parts = []
    for half in range(2):
        cols = slice(half * HD, (half + 1) * HD)
        scores = lax.dot_general(
            query_ref[:, cols],
            key_ref[:, cols],
            (((1,), (1,)), ((), ())),
            preferred_element_type=jnp.float32,
        )
        row = jnp.broadcast_to(table_ref[0, half : half + 1, :], (seq_len, 2 * seq_len))
        bias = pltpu.roll(row, 0, 1, stride=1, stride_axis=0)[:, :seq_len]
        masked = jnp.where(key_valid, scores * (1.0 / math.sqrt(HD)) + bias, -jnp.inf)
        exp_scores = jnp.exp(masked - jnp.max(masked, axis=-1, keepdims=True))
        probs = exp_scores * (1.0 / jnp.sum(exp_scores, axis=-1, keepdims=True))
        probs_ref[half] = probs
        parts.append(
            jnp.dot(
                probs.astype(jnp.bfloat16), value_ref[:, cols], preferred_element_type=jnp.float32
            ).astype(jnp.bfloat16)
        )
    context_ref[...] = jnp.concatenate(parts, axis=1)


def attn_forward(length, qkv, table):
    seq_len = qkv.shape[0]
    head_width = qkv.shape[1] // 3
    pairs = head_width // PAIR

    def column(kind):
        return pl.BlockSpec((seq_len, PAIR), lambda p: (0, kind * pairs + p))

    return pl.pallas_call(
        attn_forward_kernel,
        grid=(pairs,),
        out_shape=(
            jax.ShapeDtypeStruct((seq_len, head_width), jnp.bfloat16),
            jax.ShapeDtypeStruct((2 * pairs, seq_len, seq_len), jnp.float32),
        ),
        in_specs=[
            pl.BlockSpec(memory_space=pltpu.SMEM),
            column(0),
            column(1),
            column(2),
            pl.BlockSpec((1, 2, 2 * seq_len), lambda p: (p, 0, 0)),
        ],
        out_specs=(
            pl.BlockSpec((seq_len, PAIR), lambda p: (0, p)),
            pl.BlockSpec((2, seq_len, seq_len), lambda p: (p, 0, 0)),
        ),
        compiler_params=pltpu.CompilerParams(vmem_limit_bytes=vmem_bytes),
        cost_estimate=pl.CostEstimate(
            flops=8 * pairs * seq_len * seq_len * HD,
            bytes_accessed=8 * pairs * seq_len * seq_len,
            transcendentals=2 * pairs * seq_len * seq_len,
        ),
        name="attn_forward",
    )(length, qkv, qkv, qkv, table.reshape(pairs, 2, 2 * seq_len))


def attn_backward_kernel(
    query_ref, key_ref, value_ref, grad_ref, probs_ref, dq_ref, dk_ref, dv_ref, diag_ref
):
    seq_len = query_ref.shape[0]
    row_id = lax.broadcasted_iota(jnp.int32, (seq_len, seq_len), 0)
    col_id = lax.broadcasted_iota(jnp.int32, (seq_len, seq_len), 1)
    flip = (row_id + col_id == seq_len - 1).astype(jnp.bfloat16)
    scale = 1.0 / math.sqrt(HD)
    query_grads, key_grads, value_grads = [], [], []
    for half in range(2):
        cols = slice(half * HD, (half + 1) * HD)
        grad_context = grad_ref[:, cols]
        probs = probs_ref[half]
        value_grads.append(
            lax.dot_general(
                probs.astype(jnp.bfloat16),
                grad_context,
                (((0,), (0,)), ((), ())),
                preferred_element_type=jnp.float32,
            ).astype(jnp.bfloat16)
        )
        grad_p = lax.dot_general(
            grad_context,
            value_ref[:, cols],
            (((1,), (1,)), ((), ())),
            preferred_element_type=jnp.float32,
        )
        grad_scores = (
            probs * (grad_p - jnp.sum(probs * grad_p, axis=-1, keepdims=True))
        ).astype(jnp.bfloat16)
        query_grads.append(
            (
                jnp.dot(grad_scores, key_ref[:, cols], preferred_element_type=jnp.float32) * scale
            ).astype(jnp.bfloat16)
        )
        key_grads.append(
            (
                lax.dot_general(
                    grad_scores,
                    query_ref[:, cols],
                    (((0,), (0,)), ((), ())),
                    preferred_element_type=jnp.float32,
                )
                * scale
            ).astype(jnp.bfloat16)
        )
        reversed_cols = jnp.dot(grad_scores, flip, preferred_element_type=jnp.float32)
        wide = jnp.concatenate([reversed_cols, jnp.zeros_like(reversed_cols)], axis=1)
        skewed = pltpu.roll(wide, 0, 1, stride=1, stride_axis=0)
        diag_ref[0, half : half + 1, :] = jnp.sum(skewed, axis=0, keepdims=True)
    dq_ref[...] = jnp.concatenate(query_grads, axis=1)
    dk_ref[...] = jnp.concatenate(key_grads, axis=1)
    dv_ref[...] = jnp.concatenate(value_grads, axis=1)


def attn_backward(qkv, grad_context, probs):
    seq_len, head_width = grad_context.shape
    pairs = head_width // PAIR

    def column(kind):
        return pl.BlockSpec((seq_len, PAIR), lambda p: (0, kind * pairs + p))

    rows = jax.ShapeDtypeStruct((seq_len, head_width), jnp.bfloat16)
    dq, dk, dv, diag = pl.pallas_call(
        attn_backward_kernel,
        grid=(pairs,),
        out_shape=(rows, rows, rows, jax.ShapeDtypeStruct((pairs, 2, 2 * seq_len), jnp.float32)),
        in_specs=[
            column(0),
            column(1),
            column(2),
            column(0),
            pl.BlockSpec((2, seq_len, seq_len), lambda p: (p, 0, 0)),
        ],
        out_specs=(
            column(0),
            column(0),
            column(0),
            pl.BlockSpec((1, 2, 2 * seq_len), lambda p: (p, 0, 0)),
        ),
        compiler_params=pltpu.CompilerParams(vmem_limit_bytes=vmem_bytes),
        cost_estimate=pl.CostEstimate(
            flops=24 * pairs * seq_len * seq_len * HD,
            bytes_accessed=8 * pairs * seq_len * seq_len,
            transcendentals=0,
        ),
        name="attn_backward",
    )(qkv, qkv, qkv, grad_context, probs)
    return dq, dk, dv, diag.reshape(2 * pairs, 2 * seq_len)


def outer_kernel(left_ref, right_ref, out_ref):
    out_ref[...] = lax.dot_general(
        left_ref[...],
        right_ref[...],
        (((0,), (0,)), ((), ())),
        preferred_element_type=jnp.float32,
    ).astype(out_ref.dtype)


def expert_outer(left, right):
    rows, width = left.shape
    capacity = rows // EXP
    hidden = right.shape[1]
    tile = math.gcd(hidden, 768)
    tiles = hidden // tile
    return pl.pallas_call(
        outer_kernel,
        grid=(EXP, tiles),
        out_shape=jax.ShapeDtypeStruct((width, EXP * hidden), jnp.bfloat16),
        in_specs=[
            pl.BlockSpec((capacity, width), lambda e, t: (e, 0)),
            pl.BlockSpec((capacity, tile), lambda e, t: (e, t)),
        ],
        out_specs=pl.BlockSpec((width, tile), lambda e, t: (0, e * tiles + t)),
        compiler_params=pltpu.CompilerParams(vmem_limit_bytes=vmem_bytes),
        cost_estimate=pl.CostEstimate(
            flops=2 * rows * width * hidden,
            bytes_accessed=2 * (rows * (width + tiles * hidden) + width * EXP * hidden),
            transcendentals=0,
        ),
        name="expert_outer",
    )(left, right)


def gather_rows(shard):
    return lax.all_gather(shard, "fsdp", axis=0, tiled=True)


def scatter_rows(term):
    return lax.psum_scatter(term, "fsdp", scatter_dimension=0, tiled=True).astype(jnp.float32)


def per_device(
    tokens,
    lengths,
    routes,
    cotangent,
    gain_attn,
    gain_moe,
    qkv_weight,
    out_weight,
    rel_table,
    router_weight,
    w_in,
    w_out,
):
    tok_dev, model_width = tokens.shape
    tp_count = lax.axis_size("tp")
    seq_len = tok_dev * tp_count
    capacity = 3 * seq_len // 8
    slot_count = EXP * capacity
    heads_local = HEADS // tp_count
    hidden_local = w_in.shape[2]
    head_width = qkv_weight.shape[2]
    shard_rows = qkv_weight.shape[0]
    tp_index = lax.axis_index("tp")
    group_id = lax.axis_index("fsdp")
    length = lax.dynamic_index_in_dim(lengths, group_id, 0, keepdims=False)
    all_pos = jnp.arange(seq_len, dtype=jnp.int32)
    key_valid = all_pos < length
    local_pos = tp_index * tok_dev + jnp.arange(tok_dev, dtype=jnp.int32)
    local_valid = (local_pos < length).astype(jnp.float32)[:, None]
    expert_ids = jnp.arange(EXP, dtype=jnp.int32)
    routes_group = routes[:, 0]
    chosen = (routes_group[:, None] == expert_ids[None, :]).astype(jnp.int32) * key_valid.astype(
        jnp.int32
    )[:, None]
    own_counts = jnp.sum(chosen, axis=0).astype(jnp.bfloat16)
    small_shard = jnp.concatenate(
        [
            qkv_weight.reshape(shard_rows, 3 * head_width),
            out_weight,
            jnp.broadcast_to(jnp.pad(own_counts, (0, 128 - EXP))[None, :], (shard_rows, 128)),
        ],
        axis=1,
    )
    small_full = gather_rows(small_shard)
    qkv_full = small_full[:, : 3 * head_width]
    out_full = small_full[:, 3 * head_width : 4 * head_width]
    counts_all = jnp.sum(
        small_full[::shard_rows, 4 * head_width : 4 * head_width + EXP].astype(jnp.float32), axis=0
    )
    in_full = gather_rows(w_in)
    down_full = gather_rows(w_out)
    token_f = tokens.astype(jnp.float32)
    gain_one = gain_attn.astype(jnp.float32)
    gain_two = gain_moe.astype(jnp.float32)
    hat_attn, factor_attn, normed_attn = norm_rows(token_f, gain_one)
    attn_in = lax.all_gather(normed_attn, "tp", axis=0, tiled=True)
    qkv = jnp.dot(attn_in, qkv_full, preferred_element_type=jnp.float32).astype(jnp.bfloat16)
    table_local = lax.dynamic_slice_in_dim(rel_table, tp_index * heads_local, heads_local, 1)
    place_onehot = (
        offset_buckets(seq_len)[:, None] == jnp.arange(BUCKETS, dtype=jnp.int32)[None, :]
    )
    offset_table = jnp.einsum(
        "bh,mb->hm",
        table_local,
        place_onehot.astype(jnp.bfloat16),
        preferred_element_type=jnp.float32,
    )
    context_flat, attn_probs = attn_forward(
        jnp.reshape(length, (1,)).astype(jnp.int32), qkv, offset_table
    )
    attn_sum = lax.psum_scatter(
        lax.dot_general(
            context_flat, out_full, (((1,), (1,)), ((), ())), preferred_element_type=jnp.float32
        ),
        "tp",
        scatter_dimension=0,
        tiled=True,
    )
    mid = token_f + attn_sum * local_valid
    hat_moe, factor_moe, normed_moe = norm_rows(mid, gain_two)
    router_f = router_weight.astype(jnp.float32)
    logits = jnp.dot(normed_moe, router_weight, preferred_element_type=jnp.float32)
    router_probs = jax.nn.softmax(logits, axis=-1)
    route_local = lax.dynamic_slice_in_dim(routes_group, tp_index * tok_dev, tok_dev)
    onehot_local = (route_local[:, None] == expert_ids[None, :]).astype(jnp.float32)
    gate = jnp.sum(router_probs * onehot_local, axis=1, keepdims=True)
    prob_local = jnp.sum(local_valid * router_probs, axis=0)
    total_tokens = jnp.sum(lengths).astype(jnp.float32)
    fraction = counts_all / total_tokens
    grad_out = cotangent.astype(jnp.float32)
    scaled_grad = (grad_out * gate * local_valid).astype(jnp.bfloat16)
    moe_rows = lax.all_gather(
        jnp.concatenate([normed_moe, scaled_grad], axis=1), "tp", axis=0, tiled=True
    )
    slot_ids = jnp.sum(chosen * (jnp.cumsum(chosen, axis=0) - 1), axis=1)
    flat_index = jnp.where(key_valid, routes_group * capacity + slot_ids, slot_count)
    owner = jnp.zeros((slot_count + 1,), jnp.int32).at[flat_index].set(all_pos)[:slot_count]
    filled = (jnp.zeros((slot_count + 1,), jnp.int32).at[flat_index].set(1)[:slot_count] > 0)[
        :, None
    ]
    zero_bf = jnp.zeros((), jnp.bfloat16)
    slot_rows = jnp.where(filled, moe_rows[owner], zero_bf)
    dispatched_flat = slot_rows[:, :model_width]
    grad_expert_flat = slot_rows[:, model_width:]
    dispatched = dispatched_flat.reshape(EXP, capacity, model_width)
    grad_expert = grad_expert_flat.reshape(EXP, capacity, model_width)
    pre_act = jnp.einsum("ecd,def->ecf", dispatched, in_full, preferred_element_type=jnp.float32)
    act = jax.nn.gelu(pre_act, approximate=False).astype(jnp.bfloat16)
    expert_part = jnp.einsum("ecf,def->ecd", act, down_full, preferred_element_type=jnp.float32)
    padded_part = jnp.concatenate(
        [expert_part.reshape(slot_count, model_width), jnp.zeros((1, model_width), jnp.float32)],
        axis=0,
    )
    combined = lax.psum_scatter(
        padded_part[flat_index].astype(jnp.bfloat16), "tp", scatter_dimension=0, tiled=True
    ).astype(jnp.float32)
    mixed = (mid + gate * combined * local_valid).astype(jnp.bfloat16)
    grad_gate = jnp.sum(grad_out * combined * local_valid, axis=1, keepdims=True)
    down_sum = scatter_rows(
        expert_outer(grad_expert_flat, act.reshape(slot_count, hidden_local))
    )
    grad_act = jnp.einsum(
        "ecd,def->ecf", grad_expert, down_full, preferred_element_type=jnp.float32
    )
    _, gelu_pull = jax.vjp(lambda inner_value: jax.nn.gelu(inner_value, approximate=False), pre_act)
    grad_pre = gelu_pull(grad_act)[0].astype(jnp.bfloat16)
    in_sum = scatter_rows(
        expert_outer(dispatched_flat, grad_pre.reshape(slot_count, hidden_local))
    )
    grad_dispatch = jnp.einsum(
        "ecf,def->ecd", grad_pre, in_full, preferred_element_type=jnp.float32
    )
    padded_dispatch = jnp.concatenate(
        [grad_dispatch.reshape(slot_count, model_width), jnp.zeros((1, model_width), jnp.float32)],
        axis=0,
    )
    grad_normed = lax.psum_scatter(
        padded_dispatch[flat_index], "tp", scatter_dimension=0, tiled=True
    )
    aux_grad = balance_weight * EXP * fraction / total_tokens
    grad_probs = onehot_local * grad_gate + local_valid * aux_grad[None, :]
    grad_logits = router_probs * (
        grad_probs - jnp.sum(router_probs * grad_probs, axis=1, keepdims=True)
    )
    grad_router = jnp.einsum(
        "sd,se->de", normed_moe.astype(jnp.float32), grad_logits, precision=highest
    )
    grad_normed = grad_normed + jnp.einsum("se,de->sd", grad_logits, router_f, precision=highest)
    grad_mid_norm, grad_gain_moe = norm_back(grad_normed, hat_moe, factor_moe, gain_two)
    grad_mid = grad_out + grad_mid_norm
    grad_branch = (grad_mid * local_valid).astype(jnp.bfloat16)
    grad_branch_all = lax.all_gather(grad_branch, "tp", axis=0, tiled=True)
    grad_context = jnp.dot(grad_branch_all, out_full, preferred_element_type=jnp.float32).astype(
        jnp.bfloat16
    )
    dq, dk, dv, diag = attn_backward(qkv, grad_context, attn_probs)
    grad_qkv_rows = jnp.concatenate([dq, dk, dv], axis=1)
    grad_attn_part = lax.dot_general(
        grad_qkv_rows, qkv_full, (((1,), (1,)), ((), ())), preferred_element_type=jnp.float32
    )
    back_places = (seq_len - 1 - jnp.arange(2 * seq_len, dtype=jnp.int32)) % (2 * seq_len)
    back_onehot = (
        offset_buckets(seq_len)[back_places][:, None]
        == jnp.arange(BUCKETS, dtype=jnp.int32)[None, :]
    ).astype(jnp.float32)
    grad_table_local = jnp.einsum("hm,mb->hb", diag, back_onehot, precision=highest)
    grad_attn_in = lax.psum_scatter(
        grad_attn_part.astype(jnp.bfloat16), "tp", scatter_dimension=0, tiled=True
    ).astype(jnp.float32)
    grad_token_norm, grad_gain_attn = norm_back(grad_attn_in, hat_attn, factor_attn, gain_one)
    grad_tokens = (grad_mid + grad_token_norm).astype(jnp.bfloat16)
    table_full = lax.dynamic_update_slice(
        jnp.zeros((BUCKETS, HEADS), jnp.float32), grad_table_local.T, (0, tp_index * heads_local)
    )
    qkv_term = jnp.einsum(
        "sd,sc->dc", attn_in, grad_qkv_rows, preferred_element_type=jnp.float32
    ).astype(jnp.bfloat16)
    out_term = jnp.einsum(
        "sj,si->ji", grad_branch_all, context_flat, preferred_element_type=jnp.float32
    ).astype(jnp.bfloat16)
    small_sum = scatter_rows(jnp.concatenate([qkv_term, out_term], axis=1))
    grad_qkv = small_sum[:, : 3 * head_width].reshape(shard_rows, 3, head_width)
    grad_out_shard = small_sum[:, 3 * head_width :]
    grad_in_part = in_sum.reshape(shard_rows, EXP, hidden_local)
    grad_down_part = down_sum.reshape(shard_rows, EXP, hidden_local)
    gain_attn_sum, gain_moe_sum, router_sum, table_sum, prob_all = lax.psum(
        (grad_gain_attn, grad_gain_moe, grad_router, table_full, prob_local), ("fsdp", "tp")
    )
    balance = EXP * jnp.sum(fraction * (prob_all / total_tokens))
    return (
        mixed,
        balance,
        grad_tokens,
        gain_attn_sum,
        gain_moe_sum,
        grad_qkv,
        grad_out_shard,
        table_sum,
        router_sum,
        grad_in_part,
        grad_down_part,
    )


def solution(mesh):
    placed = (
        P(("fsdp", "tp"), None),
        P(),
        P("fsdp", None),
        P(("fsdp", "tp"), None),
        P(),
        P(),
        P("fsdp", None, "tp"),
        P("fsdp", "tp"),
        P(),
        P(),
        P("fsdp", None, "tp"),
        P("fsdp", None, "tp"),
    )
    return jax.shard_map(
        per_device,
        mesh=mesh,
        in_specs=placed,
        out_specs=(
            P(("fsdp", "tp"), None),
            P(),
            P(("fsdp", "tp"), None),
            P(),
            P(),
            P("fsdp", None, "tp"),
            P("fsdp", "tp"),
            P(),
            P(),
            P("fsdp", None, "tp"),
            P("fsdp", None, "tp"),
        ),
        check_vma=False,
    )
```

```python
import math

import jax
import jax.numpy as jnp
from jax import lax
from jax.experimental import pallas as pl
from jax.experimental.pallas import tpu as pltpu
from jax.sharding import PartitionSpec as P

HEADS = 12
HD = 64
BUCKETS = 32
EXP = 4


epsilon = 1e-06
balance_weight = 0.01
far_edges = (12, 16, 23, 32, 46, 64, 91)
highest = lax.Precision.HIGHEST


def bucket_index(query_pos, key_pos):
    offset = key_pos[None, :] - query_pos[:, None]
    spread = jnp.abs(offset)
    far_bucket = 8 + sum(((spread >= edge).astype(jnp.int32) for edge in far_edges))
    near_bucket = jnp.where(spread < 8, spread, far_bucket)
    return near_bucket + jnp.where(offset > 0, 16, 0).astype(jnp.int32)


def norm_rows(values, gain_vec):
    factor = lax.rsqrt(jnp.mean(values * values, axis=-1, keepdims=True) + epsilon)
    hat_rows = values * factor
    return (hat_rows, factor, (hat_rows * gain_vec).astype(jnp.bfloat16))


def norm_back(grad_normed, hat_rows, factor, gain_vec):
    grad_hat = grad_normed * gain_vec
    inner = jnp.mean(grad_hat * hat_rows, axis=-1, keepdims=True)
    return (factor * (grad_hat - hat_rows * inner), jnp.sum(grad_normed * hat_rows, axis=0))


PAIR = 2 * HD
vmem_bytes = 40 * 1024 * 1024


def offset_buckets(seq_len):
    places = jnp.arange(2 * seq_len, dtype=jnp.int32)
    offset = jnp.where(places < seq_len, places, places - 2 * seq_len)
    return bucket_index(jnp.zeros((1,), jnp.int32), offset)[0]


def attn_forward_kernel(len_ref, query_ref, key_ref, value_ref, table_ref, context_ref, probs_ref):
    seq_len = query_ref.shape[0]
    key_pos = lax.broadcasted_iota(jnp.int32, (1, seq_len), 1)
    key_valid = key_pos < len_ref[0]
    parts = []
    for half in range(2):
        cols = slice(half * HD, (half + 1) * HD)
        scores = lax.dot_general(
            query_ref[:, cols],
            key_ref[:, cols],
            (((1,), (1,)), ((), ())),
            preferred_element_type=jnp.float32,
        )
        row = jnp.broadcast_to(table_ref[0, half : half + 1, :], (seq_len, 2 * seq_len))
        bias = pltpu.roll(row, 0, 1, stride=1, stride_axis=0)[:, :seq_len]
        masked = jnp.where(key_valid, scores * (1.0 / math.sqrt(HD)) + bias, -jnp.inf)
        exp_scores = jnp.exp(masked - jnp.max(masked, axis=-1, keepdims=True))
        probs = exp_scores * (1.0 / jnp.sum(exp_scores, axis=-1, keepdims=True))
        probs_ref[half] = probs
        parts.append(
            jnp.dot(
                probs.astype(jnp.bfloat16), value_ref[:, cols], preferred_element_type=jnp.float32
            ).astype(jnp.bfloat16)
        )
    context_ref[...] = jnp.concatenate(parts, axis=1)


def attn_forward(length, qkv, table):
    seq_len = qkv.shape[0]
    head_width = qkv.shape[1] // 3
    pairs = head_width // PAIR

    def column(kind):
        return pl.BlockSpec((seq_len, PAIR), lambda p: (0, kind * pairs + p))

    return pl.pallas_call(
        attn_forward_kernel,
        grid=(pairs,),
        out_shape=(
            jax.ShapeDtypeStruct((seq_len, head_width), jnp.bfloat16),
            jax.ShapeDtypeStruct((2 * pairs, seq_len, seq_len), jnp.float32),
        ),
        in_specs=[
            pl.BlockSpec(memory_space=pltpu.SMEM),
            column(0),
            column(1),
            column(2),
            pl.BlockSpec((1, 2, 2 * seq_len), lambda p: (p, 0, 0)),
        ],
        out_specs=(
            pl.BlockSpec((seq_len, PAIR), lambda p: (0, p)),
            pl.BlockSpec((2, seq_len, seq_len), lambda p: (p, 0, 0)),
        ),
        compiler_params=pltpu.CompilerParams(vmem_limit_bytes=vmem_bytes),
        cost_estimate=pl.CostEstimate(
            flops=8 * pairs * seq_len * seq_len * HD,
            bytes_accessed=8 * pairs * seq_len * seq_len,
            transcendentals=2 * pairs * seq_len * seq_len,
        ),
        name="attn_forward",
    )(length, qkv, qkv, qkv, table.reshape(pairs, 2, 2 * seq_len))


def attn_backward_kernel(
    query_ref, key_ref, value_ref, grad_ref, probs_ref, dq_ref, dk_ref, dv_ref, diag_ref
):
    seq_len = query_ref.shape[0]
    row_id = lax.broadcasted_iota(jnp.int32, (seq_len, seq_len), 0)
    col_id = lax.broadcasted_iota(jnp.int32, (seq_len, seq_len), 1)
    flip = (row_id + col_id == seq_len - 1).astype(jnp.bfloat16)
    scale = 1.0 / math.sqrt(HD)
    query_grads, key_grads, value_grads = [], [], []
    for half in range(2):
        cols = slice(half * HD, (half + 1) * HD)
        grad_context = grad_ref[:, cols]
        probs = probs_ref[half]
        value_grads.append(
            lax.dot_general(
                probs.astype(jnp.bfloat16),
                grad_context,
                (((0,), (0,)), ((), ())),
                preferred_element_type=jnp.float32,
            ).astype(jnp.bfloat16)
        )
        grad_p = lax.dot_general(
            grad_context,
            value_ref[:, cols],
            (((1,), (1,)), ((), ())),
            preferred_element_type=jnp.float32,
        )
        grad_scores = (
            probs * (grad_p - jnp.sum(probs * grad_p, axis=-1, keepdims=True))
        ).astype(jnp.bfloat16)
        query_grads.append(
            (
                jnp.dot(grad_scores, key_ref[:, cols], preferred_element_type=jnp.float32) * scale
            ).astype(jnp.bfloat16)
        )
        key_grads.append(
            (
                lax.dot_general(
                    grad_scores,
                    query_ref[:, cols],
                    (((0,), (0,)), ((), ())),
                    preferred_element_type=jnp.float32,
                )
                * scale
            ).astype(jnp.bfloat16)
        )
        reversed_cols = jnp.dot(grad_scores, flip, preferred_element_type=jnp.float32)
        wide = jnp.concatenate([reversed_cols, jnp.zeros_like(reversed_cols)], axis=1)
        skewed = pltpu.roll(wide, 0, 1, stride=1, stride_axis=0)
        diag_ref[0, half : half + 1, :] = jnp.sum(skewed, axis=0, keepdims=True)
    dq_ref[...] = jnp.concatenate(query_grads, axis=1)
    dk_ref[...] = jnp.concatenate(key_grads, axis=1)
    dv_ref[...] = jnp.concatenate(value_grads, axis=1)


def attn_backward(qkv, grad_context, probs):
    seq_len, head_width = grad_context.shape
    pairs = head_width // PAIR

    def column(kind):
        return pl.BlockSpec((seq_len, PAIR), lambda p: (0, kind * pairs + p))

    rows = jax.ShapeDtypeStruct((seq_len, head_width), jnp.bfloat16)
    dq, dk, dv, diag = pl.pallas_call(
        attn_backward_kernel,
        grid=(pairs,),
        out_shape=(rows, rows, rows, jax.ShapeDtypeStruct((pairs, 2, 2 * seq_len), jnp.float32)),
        in_specs=[
            column(0),
            column(1),
            column(2),
            column(0),
            pl.BlockSpec((2, seq_len, seq_len), lambda p: (p, 0, 0)),
        ],
        out_specs=(
            column(0),
            column(0),
            column(0),
            pl.BlockSpec((1, 2, 2 * seq_len), lambda p: (p, 0, 0)),
        ),
        compiler_params=pltpu.CompilerParams(vmem_limit_bytes=vmem_bytes),
        cost_estimate=pl.CostEstimate(
            flops=24 * pairs * seq_len * seq_len * HD,
            bytes_accessed=8 * pairs * seq_len * seq_len,
            transcendentals=0,
        ),
        name="attn_backward",
    )(qkv, qkv, qkv, grad_context, probs)
    return dq, dk, dv, diag.reshape(2 * pairs, 2 * seq_len)


def outer_kernel(left_ref, right_ref, out_ref):
    out_ref[...] = lax.dot_general(
        left_ref[...],
        right_ref[...],
        (((0,), (0,)), ((), ())),
        preferred_element_type=jnp.float32,
    ).astype(out_ref.dtype)


def expert_outer(left, right, first, number):
    rows, width = left.shape
    capacity = rows // EXP
    hidden = right.shape[1]
    tile = math.gcd(hidden, 768)
    tiles = hidden // tile
    return pl.pallas_call(
        outer_kernel,
        grid=(number, tiles),
        out_shape=jax.ShapeDtypeStruct((width, number * hidden), jnp.bfloat16),
        in_specs=[
            pl.BlockSpec((capacity, width), lambda e, t: (first + e, 0)),
            pl.BlockSpec((capacity, tile), lambda e, t: (first + e, t)),
        ],
        out_specs=pl.BlockSpec((width, tile), lambda e, t: (0, e * tiles + t)),
        compiler_params=pltpu.CompilerParams(vmem_limit_bytes=vmem_bytes),
        cost_estimate=pl.CostEstimate(
            flops=2 * number * capacity * width * hidden,
            bytes_accessed=2 * number * (capacity * (width + hidden) + width * hidden),
            transcendentals=0,
        ),
        name="expert_outer",
    )(left, right)


def gather_rows(shard):
    return lax.all_gather(shard, "fsdp", axis=0, tiled=True)


def halving_masks():
    bits = lax.axis_size("fsdp").bit_length() - 1
    near = [1 << bit for bit in range(min(2, bits))]
    return near + [1 << bit for bit in range(bits - 1, 1, -1)]


def send_order(shard_rows):
    count = lax.axis_size("fsdp")
    masks = halving_masks()
    place = jnp.arange(count, dtype=jnp.int32)
    mask = jnp.zeros_like(place)
    for step, step_mask in enumerate(masks):
        bit = (place >> (len(masks) - 1 - step)) & 1
        mask = mask + bit * step_mask
    owner = mask ^ lax.axis_index("fsdp")
    source = (owner[:, None] * shard_rows + jnp.arange(shard_rows, dtype=jnp.int32)).reshape(-1)
    return (jnp.arange(count * shard_rows, dtype=jnp.int32)[:, None] == source[None, :]).astype(
        jnp.bfloat16
    )


def in_order(values, order):
    return jnp.dot(values, order, preferred_element_type=jnp.float32).astype(jnp.bfloat16)


def halve_rows(rows, step):
    count = lax.axis_size("fsdp")
    masks = halving_masks()
    half = rows.shape[0] // 2
    pairs = [(device, device ^ masks[step]) for device in range(count)]
    arrived = lax.ppermute(rows[half:], "fsdp", pairs)
    total = rows[:half].astype(jnp.float32) + arrived.astype(jnp.float32)
    return total if step == len(masks) - 1 else total.astype(jnp.bfloat16)


def finish_rows(rows, step):
    for later in range(step, len(halving_masks())):
        rows = halve_rows(rows, later)
    return rows


def per_device(
    tokens,
    lengths,
    routes,
    cotangent,
    gain_attn,
    gain_moe,
    qkv_weight,
    out_weight,
    rel_table,
    router_weight,
    w_in,
    w_out,
):
    tok_dev, model_width = tokens.shape
    tp_count = lax.axis_size("tp")
    seq_len = tok_dev * tp_count
    capacity = 3 * seq_len // 8
    slot_count = EXP * capacity
    heads_local = HEADS // tp_count
    hidden_local = w_in.shape[2]
    head_width = qkv_weight.shape[2]
    shard_rows = qkv_weight.shape[0]
    tp_index = lax.axis_index("tp")
    group_id = lax.axis_index("fsdp")
    length = lax.dynamic_index_in_dim(lengths, group_id, 0, keepdims=False)
    all_pos = jnp.arange(seq_len, dtype=jnp.int32)
    key_valid = all_pos < length
    local_pos = tp_index * tok_dev + jnp.arange(tok_dev, dtype=jnp.int32)
    local_valid = (local_pos < length).astype(jnp.float32)[:, None]
    expert_ids = jnp.arange(EXP, dtype=jnp.int32)
    routes_group = routes[:, 0]
    chosen = (routes_group[:, None] == expert_ids[None, :]).astype(jnp.int32) * key_valid.astype(
        jnp.int32
    )[:, None]
    own_counts = jnp.sum(chosen, axis=0).astype(jnp.bfloat16)
    small_shard = jnp.concatenate(
        [
            qkv_weight.reshape(shard_rows, 3 * head_width),
            out_weight,
            jnp.broadcast_to(jnp.pad(own_counts, (0, 128 - EXP))[None, :], (shard_rows, 128)),
        ],
        axis=1,
    )
    small_full = gather_rows(small_shard)
    qkv_full = small_full[:, : 3 * head_width]
    out_full = small_full[:, 3 * head_width : 4 * head_width]
    counts_all = jnp.sum(
        small_full[::shard_rows, 4 * head_width : 4 * head_width + EXP].astype(jnp.float32), axis=0
    )
    in_full = gather_rows(w_in)
    down_full = gather_rows(w_out)
    token_f = tokens.astype(jnp.float32)
    gain_one = gain_attn.astype(jnp.float32)
    gain_two = gain_moe.astype(jnp.float32)
    hat_attn, factor_attn, normed_attn = norm_rows(token_f, gain_one)
    attn_in = lax.all_gather(normed_attn, "tp", axis=0, tiled=True)
    qkv = jnp.dot(attn_in, qkv_full, preferred_element_type=jnp.float32).astype(jnp.bfloat16)
    table_local = lax.dynamic_slice_in_dim(rel_table, tp_index * heads_local, heads_local, 1)
    place_onehot = (
        offset_buckets(seq_len)[:, None] == jnp.arange(BUCKETS, dtype=jnp.int32)[None, :]
    )
    offset_table = jnp.einsum(
        "bh,mb->hm",
        table_local,
        place_onehot.astype(jnp.bfloat16),
        preferred_element_type=jnp.float32,
    )
    context_flat, attn_probs = attn_forward(
        jnp.reshape(length, (1,)).astype(jnp.int32), qkv, offset_table
    )
    attn_sum = lax.psum_scatter(
        lax.dot_general(
            context_flat, out_full, (((1,), (1,)), ((), ())), preferred_element_type=jnp.float32
        ),
        "tp",
        scatter_dimension=0,
        tiled=True,
    )
    mid = token_f + attn_sum * local_valid
    hat_moe, factor_moe, normed_moe = norm_rows(mid, gain_two)
    router_f = router_weight.astype(jnp.float32)
    logits = jnp.dot(normed_moe, router_weight, preferred_element_type=jnp.float32)
    router_probs = jax.nn.softmax(logits, axis=-1)
    route_local = lax.dynamic_slice_in_dim(routes_group, tp_index * tok_dev, tok_dev)
    onehot_local = (route_local[:, None] == expert_ids[None, :]).astype(jnp.float32)
    gate = jnp.sum(router_probs * onehot_local, axis=1, keepdims=True)
    prob_local = jnp.sum(local_valid * router_probs, axis=0)
    total_tokens = jnp.sum(lengths).astype(jnp.float32)
    fraction = counts_all / total_tokens
    grad_out = cotangent.astype(jnp.float32)
    scaled_grad = (grad_out * gate * local_valid).astype(jnp.bfloat16)
    moe_rows = lax.all_gather(
        jnp.concatenate([normed_moe, scaled_grad], axis=1), "tp", axis=0, tiled=True
    )
    slot_ids = jnp.sum(chosen * (jnp.cumsum(chosen, axis=0) - 1), axis=1)
    flat_index = jnp.where(key_valid, routes_group * capacity + slot_ids, slot_count)
    owner = jnp.zeros((slot_count + 1,), jnp.int32).at[flat_index].set(all_pos)[:slot_count]
    filled = (jnp.zeros((slot_count + 1,), jnp.int32).at[flat_index].set(1)[:slot_count] > 0)[
        :, None
    ]
    zero_bf = jnp.zeros((), jnp.bfloat16)
    slot_rows = jnp.where(filled, moe_rows[owner], zero_bf)
    dispatched_flat = slot_rows[:, :model_width]
    grad_expert_flat = slot_rows[:, model_width:]
    dispatched = dispatched_flat.reshape(EXP, capacity, model_width)
    grad_expert = grad_expert_flat.reshape(EXP, capacity, model_width)
    pre_act = jnp.einsum("ecd,def->ecf", dispatched, in_full, preferred_element_type=jnp.float32)
    act = jax.nn.gelu(pre_act, approximate=False).astype(jnp.bfloat16)
    expert_part = jnp.einsum("ecf,def->ecd", act, down_full, preferred_element_type=jnp.float32)
    padded_part = jnp.concatenate(
        [expert_part.reshape(slot_count, model_width), jnp.zeros((1, model_width), jnp.float32)],
        axis=0,
    )
    combined = lax.psum_scatter(
        padded_part[flat_index].astype(jnp.bfloat16), "tp", scatter_dimension=0, tiled=True
    ).astype(jnp.float32)
    mixed = (mid + gate * combined * local_valid).astype(jnp.bfloat16)
    grad_gate = jnp.sum(grad_out * combined * local_valid, axis=1, keepdims=True)
    order = send_order(shard_rows)
    grad_sent = in_order(grad_expert_flat, order)
    act_flat = act.reshape(slot_count, hidden_local)
    halves = (0, EXP // 2)
    down_terms = [expert_outer(grad_sent, act_flat, first, EXP // 2) for first in halves]
    down_rows = [halve_rows(term, 0) for term in down_terms]
    grad_act = jnp.einsum(
        "ecd,def->ecf", grad_expert, down_full, preferred_element_type=jnp.float32
    )
    _, gelu_pull = jax.vjp(lambda inner_value: jax.nn.gelu(inner_value, approximate=False), pre_act)
    grad_pre = gelu_pull(grad_act)[0].astype(jnp.bfloat16)
    dispatched_sent = in_order(dispatched_flat, order)
    grad_pre_flat = grad_pre.reshape(slot_count, hidden_local)
    in_terms = [expert_outer(dispatched_sent, grad_pre_flat, first, EXP // 2) for first in halves]
    in_terms, down_rows, grad_pre = lax.optimization_barrier((in_terms, down_rows, grad_pre))
    in_rows = [halve_rows(term, 0) for term in in_terms]
    down_rows = [halve_rows(rows, 1) for rows in down_rows]
    grad_dispatch = jnp.einsum(
        "ecf,def->ecd", grad_pre, in_full, preferred_element_type=jnp.float32
    )
    padded_dispatch = jnp.concatenate(
        [grad_dispatch.reshape(slot_count, model_width), jnp.zeros((1, model_width), jnp.float32)],
        axis=0,
    )
    grad_normed = lax.psum_scatter(
        padded_dispatch[flat_index], "tp", scatter_dimension=0, tiled=True
    )
    aux_grad = balance_weight * EXP * fraction / total_tokens
    grad_probs = onehot_local * grad_gate + local_valid * aux_grad[None, :]
    grad_logits = router_probs * (
        grad_probs - jnp.sum(router_probs * grad_probs, axis=1, keepdims=True)
    )
    grad_router = jnp.einsum(
        "sd,se->de", normed_moe.astype(jnp.float32), grad_logits, precision=highest
    )
    grad_normed = grad_normed + jnp.einsum("se,de->sd", grad_logits, router_f, precision=highest)
    grad_mid_norm, grad_gain_moe = norm_back(grad_normed, hat_moe, factor_moe, gain_two)
    grad_mid = grad_out + grad_mid_norm
    grad_branch = (grad_mid * local_valid).astype(jnp.bfloat16)
    grad_branch_all = lax.all_gather(grad_branch, "tp", axis=0, tiled=True)
    in_rows, down_rows, grad_branch_all = lax.optimization_barrier(
        (in_rows, down_rows, grad_branch_all)
    )
    in_rows = [halve_rows(rows, 1) for rows in in_rows]
    grad_context = jnp.dot(grad_branch_all, out_full, preferred_element_type=jnp.float32).astype(
        jnp.bfloat16
    )
    dq, dk, dv, diag = attn_backward(qkv, grad_context, attn_probs)
    grad_qkv_rows = jnp.concatenate([dq, dk, dv], axis=1)
    grad_attn_part = lax.dot_general(
        grad_qkv_rows, qkv_full, (((1,), (1,)), ((), ())), preferred_element_type=jnp.float32
    )
    back_places = (seq_len - 1 - jnp.arange(2 * seq_len, dtype=jnp.int32)) % (2 * seq_len)
    back_onehot = (
        offset_buckets(seq_len)[back_places][:, None]
        == jnp.arange(BUCKETS, dtype=jnp.int32)[None, :]
    ).astype(jnp.float32)
    grad_table_local = jnp.einsum("hm,mb->hb", diag, back_onehot, precision=highest)
    grad_attn_in = lax.psum_scatter(
        grad_attn_part.astype(jnp.bfloat16), "tp", scatter_dimension=0, tiled=True
    ).astype(jnp.float32)
    grad_token_norm, grad_gain_attn = norm_back(grad_attn_in, hat_attn, factor_attn, gain_one)
    grad_tokens = (grad_mid + grad_token_norm).astype(jnp.bfloat16)
    table_full = lax.dynamic_update_slice(
        jnp.zeros((BUCKETS, HEADS), jnp.float32), grad_table_local.T, (0, tp_index * heads_local)
    )
    qkv_term = jnp.einsum(
        "sd,sc->dc", in_order(attn_in, order), grad_qkv_rows, preferred_element_type=jnp.float32
    ).astype(jnp.bfloat16)
    out_term = jnp.einsum(
        "sj,si->ji", in_order(grad_branch_all, order), context_flat, preferred_element_type=jnp.float32
    ).astype(jnp.bfloat16)
    small_sum = finish_rows(jnp.concatenate([qkv_term, out_term], axis=1), 0)
    down_sum = jnp.concatenate([finish_rows(rows, 2) for rows in down_rows], axis=1)
    in_sum = jnp.concatenate([finish_rows(rows, 2) for rows in in_rows], axis=1)
    grad_qkv = small_sum[:, : 3 * head_width].reshape(shard_rows, 3, head_width)
    grad_out_shard = small_sum[:, 3 * head_width :]
    grad_in_part = in_sum.reshape(shard_rows, EXP, hidden_local)
    grad_down_part = down_sum.reshape(shard_rows, EXP, hidden_local)
    gain_attn_sum, gain_moe_sum, router_sum, table_sum, prob_all = lax.psum(
        (grad_gain_attn, grad_gain_moe, grad_router, table_full, prob_local), ("fsdp", "tp")
    )
    balance = EXP * jnp.sum(fraction * (prob_all / total_tokens))
    return (
        mixed,
        balance,
        grad_tokens,
        gain_attn_sum,
        gain_moe_sum,
        grad_qkv,
        grad_out_shard,
        table_sum,
        router_sum,
        grad_in_part,
        grad_down_part,
    )


def solution(mesh):
    placed = (
        P(("fsdp", "tp"), None),
        P(),
        P("fsdp", None),
        P(("fsdp", "tp"), None),
        P(),
        P(),
        P("fsdp", None, "tp"),
        P("fsdp", "tp"),
        P(),
        P(),
        P("fsdp", None, "tp"),
        P("fsdp", None, "tp"),
    )
    return jax.shard_map(
        per_device,
        mesh=mesh,
        in_specs=placed,
        out_specs=(
            P(("fsdp", "tp"), None),
            P(),
            P(("fsdp", "tp"), None),
            P(),
            P(),
            P("fsdp", None, "tp"),
            P("fsdp", "tp"),
            P(),
            P(),
            P("fsdp", None, "tp"),
            P("fsdp", None, "tp"),
        ),
        check_vma=False,
    )
```

```python
import math

import jax
import jax.numpy as jnp
from jax import lax
from jax.experimental import pallas as pl
from jax.experimental.pallas import tpu as pltpu
from jax.sharding import PartitionSpec as P

HEADS = 12
HD = 64
BUCKETS = 32
EXP = 4


epsilon = 1e-06
balance_weight = 0.01
far_edges = (12, 16, 23, 32, 46, 64, 91)
highest = lax.Precision.HIGHEST


def bucket_index(query_pos, key_pos):
    offset = key_pos[None, :] - query_pos[:, None]
    spread = jnp.abs(offset)
    far_bucket = 8 + sum(((spread >= edge).astype(jnp.int32) for edge in far_edges))
    near_bucket = jnp.where(spread < 8, spread, far_bucket)
    return near_bucket + jnp.where(offset > 0, 16, 0).astype(jnp.int32)


def norm_rows(values, gain_vec):
    factor = lax.rsqrt(jnp.mean(values * values, axis=-1, keepdims=True) + epsilon)
    hat_rows = values * factor
    return (hat_rows, factor, (hat_rows * gain_vec).astype(jnp.bfloat16))


def norm_back(grad_normed, hat_rows, factor, gain_vec):
    grad_hat = grad_normed * gain_vec
    inner = jnp.mean(grad_hat * hat_rows, axis=-1, keepdims=True)
    return (factor * (grad_hat - hat_rows * inner), jnp.sum(grad_normed * hat_rows, axis=0))


PAIR = 2 * HD
vmem_bytes = 40 * 1024 * 1024


def offset_buckets(seq_len):
    places = jnp.arange(2 * seq_len, dtype=jnp.int32)
    offset = jnp.where(places < seq_len, places, places - 2 * seq_len)
    return bucket_index(jnp.zeros((1,), jnp.int32), offset)[0]


def attn_forward_kernel(len_ref, query_ref, key_ref, value_ref, table_ref, context_ref, probs_ref):
    seq_len = query_ref.shape[0]
    key_pos = lax.broadcasted_iota(jnp.int32, (1, seq_len), 1)
    key_valid = key_pos < len_ref[0]
    parts = []
    for half in range(2):
        cols = slice(half * HD, (half + 1) * HD)
        scores = lax.dot_general(
            query_ref[:, cols],
            key_ref[:, cols],
            (((1,), (1,)), ((), ())),
            preferred_element_type=jnp.float32,
        )
        row = jnp.broadcast_to(table_ref[0, half : half + 1, :], (seq_len, 2 * seq_len))
        bias = pltpu.roll(row, 0, 1, stride=1, stride_axis=0)[:, :seq_len]
        masked = jnp.where(key_valid, scores * (1.0 / math.sqrt(HD)) + bias, -jnp.inf)
        exp_scores = jnp.exp(masked - jnp.max(masked, axis=-1, keepdims=True))
        probs = exp_scores * (1.0 / jnp.sum(exp_scores, axis=-1, keepdims=True))
        probs_ref[half] = probs
        parts.append(
            jnp.dot(
                probs.astype(jnp.bfloat16), value_ref[:, cols], preferred_element_type=jnp.float32
            ).astype(jnp.bfloat16)
        )
    context_ref[...] = jnp.concatenate(parts, axis=1)


def attn_forward(length, qkv, table):
    seq_len = qkv.shape[0]
    head_width = qkv.shape[1] // 3
    pairs = head_width // PAIR

    def column(kind):
        return pl.BlockSpec((seq_len, PAIR), lambda p: (0, kind * pairs + p))

    return pl.pallas_call(
        attn_forward_kernel,
        grid=(pairs,),
        out_shape=(
            jax.ShapeDtypeStruct((seq_len, head_width), jnp.bfloat16),
            jax.ShapeDtypeStruct((2 * pairs, seq_len, seq_len), jnp.float32),
        ),
        in_specs=[
            pl.BlockSpec(memory_space=pltpu.SMEM),
            column(0),
            column(1),
            column(2),
            pl.BlockSpec((1, 2, 2 * seq_len), lambda p: (p, 0, 0)),
        ],
        out_specs=(
            pl.BlockSpec((seq_len, PAIR), lambda p: (0, p)),
            pl.BlockSpec((2, seq_len, seq_len), lambda p: (p, 0, 0)),
        ),
        compiler_params=pltpu.CompilerParams(vmem_limit_bytes=vmem_bytes),
        cost_estimate=pl.CostEstimate(
            flops=8 * pairs * seq_len * seq_len * HD,
            bytes_accessed=8 * pairs * seq_len * seq_len,
            transcendentals=2 * pairs * seq_len * seq_len,
        ),
        name="attn_forward",
    )(length, qkv, qkv, qkv, table.reshape(pairs, 2, 2 * seq_len))


def attn_backward_kernel(
    query_ref, key_ref, value_ref, grad_ref, probs_ref, dq_ref, dk_ref, dv_ref, diag_ref
):
    seq_len = query_ref.shape[0]
    row_id = lax.broadcasted_iota(jnp.int32, (seq_len, seq_len), 0)
    col_id = lax.broadcasted_iota(jnp.int32, (seq_len, seq_len), 1)
    flip = (row_id + col_id == seq_len - 1).astype(jnp.bfloat16)
    scale = 1.0 / math.sqrt(HD)
    query_grads, key_grads, value_grads = [], [], []
    for half in range(2):
        cols = slice(half * HD, (half + 1) * HD)
        grad_context = grad_ref[:, cols]
        probs = probs_ref[half]
        value_grads.append(
            lax.dot_general(
                probs.astype(jnp.bfloat16),
                grad_context,
                (((0,), (0,)), ((), ())),
                preferred_element_type=jnp.float32,
            ).astype(jnp.bfloat16)
        )
        grad_p = lax.dot_general(
            grad_context,
            value_ref[:, cols],
            (((1,), (1,)), ((), ())),
            preferred_element_type=jnp.float32,
        )
        grad_scores = (
            probs * (grad_p - jnp.sum(probs * grad_p, axis=-1, keepdims=True))
        ).astype(jnp.bfloat16)
        query_grads.append(
            (
                jnp.dot(grad_scores, key_ref[:, cols], preferred_element_type=jnp.float32) * scale
            ).astype(jnp.bfloat16)
        )
        key_grads.append(
            (
                lax.dot_general(
                    grad_scores,
                    query_ref[:, cols],
                    (((0,), (0,)), ((), ())),
                    preferred_element_type=jnp.float32,
                )
                * scale
            ).astype(jnp.bfloat16)
        )
        reversed_cols = jnp.dot(grad_scores, flip, preferred_element_type=jnp.float32)
        wide = jnp.concatenate([reversed_cols, jnp.zeros_like(reversed_cols)], axis=1)
        skewed = pltpu.roll(wide, 0, 1, stride=1, stride_axis=0)
        diag_ref[0, half : half + 1, :] = jnp.sum(skewed, axis=0, keepdims=True)
    dq_ref[...] = jnp.concatenate(query_grads, axis=1)
    dk_ref[...] = jnp.concatenate(key_grads, axis=1)
    dv_ref[...] = jnp.concatenate(value_grads, axis=1)


def attn_backward(qkv, grad_context, probs):
    seq_len, head_width = grad_context.shape
    pairs = head_width // PAIR

    def column(kind):
        return pl.BlockSpec((seq_len, PAIR), lambda p: (0, kind * pairs + p))

    rows = jax.ShapeDtypeStruct((seq_len, head_width), jnp.bfloat16)
    dq, dk, dv, diag = pl.pallas_call(
        attn_backward_kernel,
        grid=(pairs,),
        out_shape=(rows, rows, rows, jax.ShapeDtypeStruct((pairs, 2, 2 * seq_len), jnp.float32)),
        in_specs=[
            column(0),
            column(1),
            column(2),
            column(0),
            pl.BlockSpec((2, seq_len, seq_len), lambda p: (p, 0, 0)),
        ],
        out_specs=(
            column(0),
            column(0),
            column(0),
            pl.BlockSpec((1, 2, 2 * seq_len), lambda p: (p, 0, 0)),
        ),
        compiler_params=pltpu.CompilerParams(vmem_limit_bytes=vmem_bytes),
        cost_estimate=pl.CostEstimate(
            flops=24 * pairs * seq_len * seq_len * HD,
            bytes_accessed=8 * pairs * seq_len * seq_len,
            transcendentals=0,
        ),
        name="attn_backward",
    )(qkv, qkv, qkv, grad_context, probs)
    return dq, dk, dv, diag.reshape(2 * pairs, 2 * seq_len)


def outer_kernel(left_ref, right_ref, out_ref):
    out_ref[...] = lax.dot_general(
        left_ref[...],
        right_ref[...],
        (((0,), (0,)), ((), ())),
        preferred_element_type=jnp.float32,
    ).astype(out_ref.dtype)


def expert_outer(left, right, first, number):
    rows, width = left.shape
    capacity = rows // EXP
    hidden = right.shape[1]
    tile = math.gcd(hidden, 768)
    tiles = hidden // tile
    return pl.pallas_call(
        outer_kernel,
        grid=(number, tiles),
        out_shape=jax.ShapeDtypeStruct((width, number * hidden), jnp.bfloat16),
        in_specs=[
            pl.BlockSpec((capacity, width), lambda e, t: (first + e, 0)),
            pl.BlockSpec((capacity, tile), lambda e, t: (first + e, t)),
        ],
        out_specs=pl.BlockSpec((width, tile), lambda e, t: (0, e * tiles + t)),
        compiler_params=pltpu.CompilerParams(vmem_limit_bytes=vmem_bytes),
        cost_estimate=pl.CostEstimate(
            flops=2 * number * capacity * width * hidden,
            bytes_accessed=2 * number * (capacity * (width + hidden) + width * hidden),
            transcendentals=0,
        ),
        name="expert_outer",
    )(left, right)


def gather_rows(shard):
    return lax.all_gather(shard, "fsdp", axis=0, tiled=True)


def halving_masks():
    bits = lax.axis_size("fsdp").bit_length() - 1
    near = [1 << bit for bit in range(min(2, bits))]
    return near + [1 << bit for bit in range(bits - 1, 1, -1)]


def send_order(shard_rows):
    count = lax.axis_size("fsdp")
    masks = halving_masks()
    place = jnp.arange(count, dtype=jnp.int32)
    mask = jnp.zeros_like(place)
    for step, step_mask in enumerate(masks):
        bit = (place >> (len(masks) - 1 - step)) & 1
        mask = mask + bit * step_mask
    owner = mask ^ lax.axis_index("fsdp")
    source = (owner[:, None] * shard_rows + jnp.arange(shard_rows, dtype=jnp.int32)).reshape(-1)
    return (jnp.arange(count * shard_rows, dtype=jnp.int32)[:, None] == source[None, :]).astype(
        jnp.bfloat16
    )


def in_order(values, order):
    return jnp.dot(values, order, preferred_element_type=jnp.float32).astype(jnp.bfloat16)


def halve_rows(rows, step):
    count = lax.axis_size("fsdp")
    masks = halving_masks()
    half = rows.shape[0] // 2
    pairs = [(device, device ^ masks[step]) for device in range(count)]
    arrived = lax.ppermute(rows[half:], "fsdp", pairs)
    total = rows[:half].astype(jnp.float32) + arrived.astype(jnp.float32)
    return total if step == len(masks) - 1 else total.astype(jnp.bfloat16)


def finish_rows(rows, step):
    for later in range(step, len(halving_masks())):
        rows = halve_rows(rows, later)
    return rows


swap = [(0, 1), (1, 0)]


def tp_gather(rows):
    if lax.axis_size("tp") != 2:
        return lax.all_gather(rows, "tp", axis=0, tiled=True)
    arrived = lax.ppermute(rows, "tp", swap)
    first = lax.axis_index("tp") == 0
    return jnp.concatenate(
        [jnp.where(first, rows, arrived), jnp.where(first, arrived, rows)], axis=0
    )


def tp_scatter(rows):
    if lax.axis_size("tp") != 2:
        return lax.psum_scatter(rows, "tp", scatter_dimension=0, tiled=True).astype(jnp.float32)
    half = rows.shape[0] // 2
    own = lax.axis_index("tp") * half
    arrived = lax.ppermute(lax.dynamic_slice_in_dim(rows, half - own, half), "tp", swap)
    kept = lax.dynamic_slice_in_dim(rows, own, half)
    return kept.astype(jnp.float32) + arrived.astype(jnp.float32)


def sum_all(values):
    sizes = [value.size for value in values]
    packed = jnp.concatenate([value.reshape(-1) for value in values])
    packed = jnp.pad(packed, (0, -packed.size % 1024)).reshape(-1, 128)
    for axis in ("tp", "fsdp"):
        count = lax.axis_size(axis)
        for bit in range(count.bit_length() - 1):
            pairs = [(device, device ^ (1 << bit)) for device in range(count)]
            packed = packed + lax.ppermute(packed, axis, pairs)
    packed = packed.reshape(-1)
    results, start = [], 0
    for value, size in zip(values, sizes):
        results.append(packed[start : start + size].reshape(value.shape))
        start += size
    return results


def per_device(
    tokens,
    lengths,
    routes,
    cotangent,
    gain_attn,
    gain_moe,
    qkv_weight,
    out_weight,
    rel_table,
    router_weight,
    w_in,
    w_out,
):
    tok_dev, model_width = tokens.shape
    tp_count = lax.axis_size("tp")
    seq_len = tok_dev * tp_count
    capacity = 3 * seq_len // 8
    slot_count = EXP * capacity
    heads_local = HEADS // tp_count
    hidden_local = w_in.shape[2]
    head_width = qkv_weight.shape[2]
    shard_rows = qkv_weight.shape[0]
    tp_index = lax.axis_index("tp")
    group_id = lax.axis_index("fsdp")
    length = lax.dynamic_index_in_dim(lengths, group_id, 0, keepdims=False)
    all_pos = jnp.arange(seq_len, dtype=jnp.int32)
    key_valid = all_pos < length
    local_pos = tp_index * tok_dev + jnp.arange(tok_dev, dtype=jnp.int32)
    local_valid = (local_pos < length).astype(jnp.float32)[:, None]
    expert_ids = jnp.arange(EXP, dtype=jnp.int32)
    routes_group = routes[:, 0]
    chosen = (routes_group[:, None] == expert_ids[None, :]).astype(jnp.int32) * key_valid.astype(
        jnp.int32
    )[:, None]
    own_counts = jnp.sum(chosen, axis=0).astype(jnp.bfloat16)
    small_shard = jnp.concatenate(
        [
            qkv_weight.reshape(shard_rows, 3 * head_width),
            out_weight,
            jnp.broadcast_to(jnp.pad(own_counts, (0, 128 - EXP))[None, :], (shard_rows, 128)),
        ],
        axis=1,
    )
    small_full = gather_rows(small_shard)
    qkv_full = small_full[:, : 3 * head_width]
    out_full = small_full[:, 3 * head_width : 4 * head_width]
    counts_all = jnp.sum(
        small_full[::shard_rows, 4 * head_width : 4 * head_width + EXP].astype(jnp.float32), axis=0
    )
    in_full = gather_rows(w_in)
    down_full = gather_rows(w_out)
    token_f = tokens.astype(jnp.float32)
    gain_one = gain_attn.astype(jnp.float32)
    gain_two = gain_moe.astype(jnp.float32)
    hat_attn, factor_attn, normed_attn = norm_rows(token_f, gain_one)
    attn_in = tp_gather(normed_attn)
    qkv = jnp.dot(attn_in, qkv_full, preferred_element_type=jnp.float32).astype(jnp.bfloat16)
    table_local = lax.dynamic_slice_in_dim(rel_table, tp_index * heads_local, heads_local, 1)
    place_onehot = (
        offset_buckets(seq_len)[:, None] == jnp.arange(BUCKETS, dtype=jnp.int32)[None, :]
    )
    offset_table = jnp.einsum(
        "bh,mb->hm",
        table_local,
        place_onehot.astype(jnp.bfloat16),
        preferred_element_type=jnp.float32,
    )
    context_flat, attn_probs = attn_forward(
        jnp.reshape(length, (1,)).astype(jnp.int32), qkv, offset_table
    )
    attn_sum = tp_scatter(
        lax.dot_general(
            context_flat, out_full, (((1,), (1,)), ((), ())), preferred_element_type=jnp.float32
        )
    )
    mid = token_f + attn_sum * local_valid
    hat_moe, factor_moe, normed_moe = norm_rows(mid, gain_two)
    router_f = router_weight.astype(jnp.float32)
    logits = jnp.dot(normed_moe, router_weight, preferred_element_type=jnp.float32)
    router_probs = jax.nn.softmax(logits, axis=-1)
    route_local = lax.dynamic_slice_in_dim(routes_group, tp_index * tok_dev, tok_dev)
    onehot_local = (route_local[:, None] == expert_ids[None, :]).astype(jnp.float32)
    gate = jnp.sum(router_probs * onehot_local, axis=1, keepdims=True)
    prob_local = jnp.sum(local_valid * router_probs, axis=0)
    total_tokens = jnp.sum(lengths).astype(jnp.float32)
    fraction = counts_all / total_tokens
    grad_out = cotangent.astype(jnp.float32)
    scaled_grad = (grad_out * gate * local_valid).astype(jnp.bfloat16)
    moe_rows = tp_gather(jnp.concatenate([normed_moe, scaled_grad], axis=1))
    slot_ids = jnp.sum(chosen * (jnp.cumsum(chosen, axis=0) - 1), axis=1)
    flat_index = jnp.where(key_valid, routes_group * capacity + slot_ids, slot_count)
    owner = jnp.zeros((slot_count + 1,), jnp.int32).at[flat_index].set(all_pos)[:slot_count]
    filled = (jnp.zeros((slot_count + 1,), jnp.int32).at[flat_index].set(1)[:slot_count] > 0)[
        :, None
    ]
    zero_bf = jnp.zeros((), jnp.bfloat16)
    slot_rows = jnp.where(filled, moe_rows[owner], zero_bf)
    dispatched_flat = slot_rows[:, :model_width]
    grad_expert_flat = slot_rows[:, model_width:]
    dispatched = dispatched_flat.reshape(EXP, capacity, model_width)
    grad_expert = grad_expert_flat.reshape(EXP, capacity, model_width)
    pre_act = jnp.einsum("ecd,def->ecf", dispatched, in_full, preferred_element_type=jnp.float32)
    act = jax.nn.gelu(pre_act, approximate=False).astype(jnp.bfloat16)
    expert_part = jnp.einsum("ecf,def->ecd", act, down_full, preferred_element_type=jnp.float32)
    padded_part = jnp.concatenate(
        [expert_part.reshape(slot_count, model_width), jnp.zeros((1, model_width), jnp.float32)],
        axis=0,
    )
    combined = tp_scatter(padded_part[flat_index].astype(jnp.bfloat16))
    mixed = (mid + gate * combined * local_valid).astype(jnp.bfloat16)
    grad_gate = jnp.sum(grad_out * combined * local_valid, axis=1, keepdims=True)
    order = send_order(shard_rows)
    grad_sent = in_order(grad_expert_flat, order)
    act_flat = act.reshape(slot_count, hidden_local)
    halves = (0, EXP // 2)
    down_terms = [expert_outer(grad_sent, act_flat, first, EXP // 2) for first in halves]
    down_rows = [halve_rows(term, 0) for term in down_terms]
    grad_act = jnp.einsum(
        "ecd,def->ecf", grad_expert, down_full, preferred_element_type=jnp.float32
    )
    _, gelu_pull = jax.vjp(lambda inner_value: jax.nn.gelu(inner_value, approximate=False), pre_act)
    grad_pre = gelu_pull(grad_act)[0].astype(jnp.bfloat16)
    dispatched_sent = in_order(dispatched_flat, order)
    grad_pre_flat = grad_pre.reshape(slot_count, hidden_local)
    in_terms = [expert_outer(dispatched_sent, grad_pre_flat, first, EXP // 2) for first in halves]
    in_terms, down_rows, grad_pre = lax.optimization_barrier((in_terms, down_rows, grad_pre))
    in_rows = [halve_rows(term, 0) for term in in_terms]
    down_rows = [halve_rows(rows, 1) for rows in down_rows]
    grad_dispatch = jnp.einsum(
        "ecf,def->ecd", grad_pre, in_full, preferred_element_type=jnp.float32
    )
    padded_dispatch = jnp.concatenate(
        [grad_dispatch.reshape(slot_count, model_width), jnp.zeros((1, model_width), jnp.float32)],
        axis=0,
    )
    grad_normed = tp_scatter(padded_dispatch[flat_index])
    aux_grad = balance_weight * EXP * fraction / total_tokens
    grad_probs = onehot_local * grad_gate + local_valid * aux_grad[None, :]
    grad_logits = router_probs * (
        grad_probs - jnp.sum(router_probs * grad_probs, axis=1, keepdims=True)
    )
    grad_router = jnp.einsum(
        "sd,se->de", normed_moe.astype(jnp.float32), grad_logits, precision=highest
    )
    grad_normed = grad_normed + jnp.einsum("se,de->sd", grad_logits, router_f, precision=highest)
    grad_mid_norm, grad_gain_moe = norm_back(grad_normed, hat_moe, factor_moe, gain_two)
    grad_mid = grad_out + grad_mid_norm
    grad_branch = (grad_mid * local_valid).astype(jnp.bfloat16)
    grad_branch_all = tp_gather(grad_branch)
    in_rows, down_rows, grad_branch_all = lax.optimization_barrier(
        (in_rows, down_rows, grad_branch_all)
    )
    in_rows = [halve_rows(rows, 1) for rows in in_rows]
    grad_context = jnp.dot(grad_branch_all, out_full, preferred_element_type=jnp.float32).astype(
        jnp.bfloat16
    )
    dq, dk, dv, diag = attn_backward(qkv, grad_context, attn_probs)
    grad_qkv_rows = jnp.concatenate([dq, dk, dv], axis=1)
    grad_attn_part = lax.dot_general(
        grad_qkv_rows, qkv_full, (((1,), (1,)), ((), ())), preferred_element_type=jnp.float32
    )
    back_places = (seq_len - 1 - jnp.arange(2 * seq_len, dtype=jnp.int32)) % (2 * seq_len)
    back_onehot = (
        offset_buckets(seq_len)[back_places][:, None]
        == jnp.arange(BUCKETS, dtype=jnp.int32)[None, :]
    ).astype(jnp.float32)
    grad_table_local = jnp.einsum("hm,mb->hb", diag, back_onehot, precision=highest)
    grad_attn_in = tp_scatter(grad_attn_part.astype(jnp.bfloat16))
    grad_token_norm, grad_gain_attn = norm_back(grad_attn_in, hat_attn, factor_attn, gain_one)
    grad_tokens = (grad_mid + grad_token_norm).astype(jnp.bfloat16)
    table_full = lax.dynamic_update_slice(
        jnp.zeros((BUCKETS, HEADS), jnp.float32), grad_table_local.T, (0, tp_index * heads_local)
    )
    qkv_term = jnp.einsum(
        "sd,sc->dc", in_order(attn_in, order), grad_qkv_rows, preferred_element_type=jnp.float32
    ).astype(jnp.bfloat16)
    out_term = jnp.einsum(
        "sj,si->ji", in_order(grad_branch_all, order), context_flat, preferred_element_type=jnp.float32
    ).astype(jnp.bfloat16)
    small_sum = finish_rows(jnp.concatenate([qkv_term, out_term], axis=1), 0)
    down_sum = jnp.concatenate([finish_rows(rows, 2) for rows in down_rows], axis=1)
    in_sum = jnp.concatenate([finish_rows(rows, 2) for rows in in_rows], axis=1)
    grad_qkv = small_sum[:, : 3 * head_width].reshape(shard_rows, 3, head_width)
    grad_out_shard = small_sum[:, 3 * head_width :]
    grad_in_part = in_sum.reshape(shard_rows, EXP, hidden_local)
    grad_down_part = down_sum.reshape(shard_rows, EXP, hidden_local)
    gain_attn_sum, gain_moe_sum, router_sum, table_sum, prob_all = sum_all(
        (grad_gain_attn, grad_gain_moe, grad_router, table_full, prob_local)
    )
    balance = EXP * jnp.sum(fraction * (prob_all / total_tokens))
    return (
        mixed,
        balance,
        grad_tokens,
        gain_attn_sum,
        gain_moe_sum,
        grad_qkv,
        grad_out_shard,
        table_sum,
        router_sum,
        grad_in_part,
        grad_down_part,
    )


def solution(mesh):
    placed = (
        P(("fsdp", "tp"), None),
        P(),
        P("fsdp", None),
        P(("fsdp", "tp"), None),
        P(),
        P(),
        P("fsdp", None, "tp"),
        P("fsdp", "tp"),
        P(),
        P(),
        P("fsdp", None, "tp"),
        P("fsdp", None, "tp"),
    )
    return jax.shard_map(
        per_device,
        mesh=mesh,
        in_specs=placed,
        out_specs=(
            P(("fsdp", "tp"), None),
            P(),
            P(("fsdp", "tp"), None),
            P(),
            P(),
            P("fsdp", None, "tp"),
            P("fsdp", "tp"),
            P(),
            P(),
            P("fsdp", None, "tp"),
            P("fsdp", None, "tp"),
        ),
        check_vma=False,
    )
```
